32 devices in a mesh: groups: 2 (over x), gx: 16 (over z, y, core).
Axes of the slice: x: 2, y: 2, z: 4, core: 2. Of those that a mesh axis runs over, the one named last changes fastest.
Arguments:
- east_current: float32 [512, 32], P(('groups', 'gx')), parts along dimension 0, may hold values from -0.2 to 0.2
- north_current: float32 [512, 32], P(('groups', 'gx')), parts along dimension 0, may hold values from -0.2 to 0.2
- land_mask: int32 [512, 32], P(('groups', 'gx')), parts along dimension 0, may hold values 0 or 1
- spectrum: bfloat16 [1296, 64, 256], P(None, ('groups', 'gx')), parts along dimension 1, may hold values from 0.049804688 to 1
- spectral_in: bfloat16 [256, 1296], replicated, may hold values from -0.15625 to 0.15625
- spectral_out: bfloat16 [1296, 256], replicated, may hold values from -0.375 to 0.375
- conv_first: bfloat16 [64, 18], replicated, may hold values from -1.5 to 1.5
- conv_second: bfloat16 [64, 576], replicated, may hold values from -0.25 to 0.25
- conv_last: bfloat16 [2, 64], replicated, may hold values from -0.75 to 0.75
Outputs:
- east_next: float32 [512, 32], P(('groups', 'gx')), parts along dimension 0
- north_next: float32 [512, 32], P(('groups', 'gx')), parts along dimension 0
- new_spectrum: bfloat16 [1296, 64, 256], P(None, ('groups', 'gx')), parts along dimension 1
The draws below stay inside these ranges and needn't reach their ends.
There are 2 independent parts, one for each index of `groups`. The reference program is written for one: setup_inputs(seed, part) draws one part's arguments, and reference() takes and returns one part's arrays. A program takes and returns all parts, laid end to end along the dimension named above; an argument that names none is the same for every part. Nothing has to cross between parts.
All inputs are finite; a program needn't handle non-finite values. No bound on the sum of `land_mask` on one device may be relied on, other than what follows from the above.
Results may differ from the reference program's by a relative error of at most 0.0052.
Values may be sent and summed in bfloat16 or wider, within the bound.
A program may use at most 256 MiB of HBM per device.

```python
import math
import jax
import jax.numpy as jnp
from jax import lax

DIRS = 36
FRQS = 36
BINS = 1296
HID = 256
HC = 64
NY = 256
NX = 32


def place_ends(array, key, smallest, high):
    longest = array.shape.index(max(array.shape))
    spots = []
    for shift in (0, 1):
        where = [jax.random.randint(jax.random.fold_in(key, axis), (), 0, length) for axis, length in enumerate(array.shape)]
        where[longest] = (where[longest] + shift) % array.shape[longest]
        spots.append(tuple(where))
    return array.at[spots[0]].set(smallest).at[spots[1]].set(high)


def levels(own_key, shape, split, least, top_value):
    factor_of = 1.0
    for dim, blocks in split:
        draws = jax.random.uniform(jax.random.fold_in(jax.random.fold_in(own_key, 6), dim), (blocks,), jnp.float32, least / len(split), top_value / len(split))
        factor_of = factor_of * jnp.repeat(jnp.exp(draws), shape[dim] // blocks).reshape((-1,) + (1,) * (len(shape) - 1 - dim))
    return factor_of


def scatter_about(rng, dims, spread, bound, held_as=jnp.bfloat16):
    array = jax.random.normal(rng, dims, jnp.float32) * spread
    return jnp.minimum(jnp.maximum(array, -bound), bound).astype(held_as)


def setup_inputs(seed: int = 0, part: int = 0) -> dict:
    streams_of = jax.random.split(jax.random.key(seed), 10)
    part_splits = jax.random.split(jax.random.fold_in(streams_of[9], part), 10)
    return {
        "east_current": jnp.clip(jax.random.uniform(part_splits[0], (NY, NX), jnp.float32, -0.2, 0.2) * levels(part_splits[0], (NY, NX), ((0, 16),), -0.4, 0.0), -0.2, 0.2),
        "north_current": jnp.clip(jax.random.uniform(part_splits[1], (NY, NX), jnp.float32, -0.2, 0.2) * levels(part_splits[1], (NY, NX), ((0, 16),), -0.4, 0.0), -0.2, 0.2),
        "land_mask": place_ends((jax.random.randint(part_splits[2], (NY, NX), 0, 10) < 7).astype(jnp.int32), jax.random.fold_in(part_splits[2], 1), 0, 1),
        "spectrum": jnp.clip(jnp.exp(math.log(1.0) - 2.9996462 * jax.random.uniform(part_splits[3], (BINS, NX, NY), jnp.float32) ** levels(part_splits[3], (BINS, NX, NY), ((1, 16),), -0.2, 0.2)), 0.049804688, 1.0).astype(jnp.bfloat16),
        "spectral_in": scatter_about(streams_of[4], (HID, BINS), BINS ** -0.5, 0.15625),
        "spectral_out": scatter_about(streams_of[5], (BINS, HID), HID ** -0.5, 0.375),
        "conv_first": scatter_about(streams_of[6], (HC, 18), 18 ** -0.5, 1.5),
        "conv_second": scatter_about(streams_of[7], (HC, 9 * HC), (9 * HC) ** -0.5, 0.25),
        "conv_last": scatter_about(streams_of[8], (2, HC), HC ** -0.5, 0.75),
    }


VISCOSITY = 0.1
CORIOLIS = 0.3
INPUT_SCALE = 5.0
SOURCE_STEP = 1.0
SPEED_MAX = 0.25

def bin_tables():
    index = jnp.arange(DIRS * FRQS, dtype=jnp.int32)
    heading = (index // FRQS).astype(jnp.float32)
    level = (index % FRQS).astype(jnp.float32)
    theta = (heading + 0.5) * (2.0 * math.pi / DIRS)
    speed = SPEED_MAX * jnp.exp(-math.log(1.1) * level)
    factor = 2.0 / math.sqrt(DIRS * FRQS)
    cosine = jnp.cos(theta)
    sine = jnp.sin(theta)
    speeds = jnp.stack([speed * cosine, speed * sine])
    drift_rows = jnp.stack([cosine, sine]) * (factor * (1.0 + level / FRQS))
    stress_rows = jnp.stack([cosine, sine]) * factor
    return (speeds, drift_rows, stress_rows)

def divergence(energy, speed, axis):
    count = energy.shape[axis] - 1
    lower_energy = lax.slice_in_dim(energy, 0, count, axis=axis)
    upper_energy = lax.slice_in_dim(energy, 1, count + 1, axis=axis)
    lower_speed = lax.slice_in_dim(speed, 0, count, axis=axis)
    upper_speed = lax.slice_in_dim(speed, 1, count + 1, axis=axis)
    flux = jnp.maximum(lower_speed, 0.0) * lower_energy + jnp.minimum(upper_speed, 0.0) * upper_energy
    return lax.slice_in_dim(flux, 1, count, axis=axis) - lax.slice_in_dim(flux, 0, count - 1, axis=axis)

def wave_step(packed, spectral_in, spectral_out, speeds):
    bins = speeds.shape[1]
    spectral = packed[:bins]
    currents = packed[bins:].astype(jnp.float32)
    inner = spectral[:, 1:-1]
    hidden = jax.nn.gelu(jnp.dot(spectral_in, inner.reshape(bins, -1), preferred_element_type=jnp.float32)).astype(jnp.bfloat16)
    source = jnp.dot(spectral_out, hidden, preferred_element_type=jnp.float32).reshape(inner.shape)
    energy = spectral.astype(jnp.float32)
    along_x = divergence(energy, speeds[0][:, None, None] + currents[0][None], 1)
    energy_in = energy[:, 1:-1]
    pad_rows = ((0, 0), (0, 0), (1, 1))
    speed_rows = speeds[1][:, None, None] + currents[1][None, 1:-1]
    along_y = divergence(jnp.pad(energy_in, pad_rows), jnp.pad(speed_rows, pad_rows), 2)
    updated = currents[2][None, 1:-1] * (energy_in - (along_x + along_y) + SOURCE_STEP * source)
    return (updated.astype(jnp.bfloat16), source)

def conv_layer(weights, inputs):
    rows = inputs.shape[1] - 2
    width = inputs.shape[2]
    padded = jnp.pad(inputs, ((0, 0), (0, 0), (1, 1)))
    taps = [padded[:, 1 + row_step:1 + row_step + rows, 1 + col_step:1 + col_step + width] for row_step in (-1, 0, 1) for col_step in (-1, 0, 1)]
    stacked = jnp.concatenate(taps, axis=0)
    total = jnp.dot(weights, stacked.reshape(stacked.shape[0], -1), preferred_element_type=jnp.float32)
    return total.reshape(weights.shape[0], rows, width)

def laplacian(fields):
    rows = fields.shape[1] - 2
    padded = jnp.pad(fields, ((0, 0), (0, 0), (1, 1)))
    center = padded[:, 1:1 + rows, 1:-1]
    beside_all = padded[:, :rows, 1:-1] + padded[:, 2:2 + rows, 1:-1] + padded[:, 1:1 + rows, :-2] + padded[:, 1:1 + rows, 2:]
    return beside_all - 4.0 * center

def reference(east_current, north_current, land_mask, spectrum, spectral_in, spectral_out, conv_first, conv_second, conv_last):
    sea = land_mask.astype(jnp.float32)
    masked = jnp.stack([east_current * sea, north_current * sea])
    coupled = jnp.concatenate([masked, sea[None]], axis=0).astype(jnp.bfloat16).transpose(0, 2, 1)
    speeds, drift_rows, stress_rows = bin_tables()
    pad_cols = ((0, 0), (1, 1), (0, 0))
    packed = jnp.pad(jnp.concatenate([spectrum, coupled], axis=0), pad_cols)
    first, unused = wave_step(packed, spectral_in, spectral_out, speeds)
    packed = jnp.pad(jnp.concatenate([first, coupled], axis=0), pad_cols)
    final, source = wave_step(packed, spectral_in, spectral_out, speeds)
    bins = DIRS * FRQS
    drift = jnp.dot(drift_rows, final.astype(jnp.float32).reshape(bins, -1), precision=lax.Precision.HIGHEST)
    stress = jnp.dot(stress_rows, source.reshape(bins, -1), precision=lax.Precision.HIGHEST)
    forcing = jnp.concatenate([drift, stress], axis=0).reshape(4, NX, NY).transpose(0, 2, 1)
    pad_rows = ((0, 0), (1, 1), (0, 0))
    scaled = (INPUT_SCALE * masked).astype(jnp.bfloat16)
    first_hidden = jax.nn.relu(conv_layer(conv_first, jnp.pad(scaled, pad_rows))).astype(jnp.bfloat16)
    second_hidden = jax.nn.relu(conv_layer(conv_second, jnp.pad(first_hidden, pad_rows))).astype(jnp.bfloat16)
    closure = jnp.dot(conv_last, second_hidden.reshape(second_hidden.shape[0], -1), preferred_element_type=jnp.float32).reshape(2, NY, NX)
    bend = laplacian(jnp.pad(masked, pad_rows))
    east_next = sea * (masked[0] + VISCOSITY * bend[0] + CORIOLIS * (masked[1] + forcing[1]) + forcing[2] + closure[0])
    north_next = sea * (masked[1] + VISCOSITY * bend[1] - CORIOLIS * (masked[0] + forcing[0]) + forcing[3] + closure[1])
    return (east_next, north_next, final)
```

```python
import functools
import math

import jax
import jax.numpy as jnp
import ml_dtypes
import numpy as np
from jax import lax
from jax.experimental import pallas as pl
from jax.experimental.pallas import tpu as pltpu
from jax.sharding import PartitionSpec as P

DIRS = 36
FRQS = 36
BINS = DIRS * FRQS
VISCOSITY = 0.1
CORIOLIS = 0.3
INPUT_SCALE = 5.0
SOURCE_STEP = 1.0
SPEED_MAX = 0.25

CHUNKS = 9
CHUNK = BINS // CHUNKS
BLOCK = 16
LANES = 128
MESH = pl.DeviceIdType.MESH
F32 = jnp.float32
BF16 = jnp.bfloat16
HIGHEST = lax.Precision.HIGHEST


def split_rows(row):
    pieces = []
    rest = row.astype(np.float32)
    for _ in range(3):
        piece = rest.astype(ml_dtypes.bfloat16)
        pieces.append(piece)
        rest = rest - piece.astype(np.float32)
    return pieces


def bin_tables():
    index = np.arange(BINS)
    heading = (index // FRQS).astype(np.float64)
    level = (index % FRQS).astype(np.float64)
    theta = (heading + 0.5) * (2.0 * math.pi / DIRS)
    speed = SPEED_MAX * np.exp(-math.log(1.1) * level)
    factor = 2.0 / math.sqrt(BINS)
    cosine, sine = np.cos(theta), np.sin(theta)
    speeds = np.stack([speed * cosine, speed * sine], axis=1).astype(np.float32)
    weight = factor * (1.0 + level / FRQS)
    drift = np.zeros((16, BINS), ml_dtypes.bfloat16)
    drift[0:3] = split_rows(cosine * weight)
    drift[3:6] = split_rows(sine * weight)
    stress = np.zeros((16, BINS), ml_dtypes.bfloat16)
    stress[0:3] = split_rows(cosine * factor)
    stress[3:6] = split_rows(sine * factor)
    drift = np.ascontiguousarray(drift.reshape(16, CHUNKS, CHUNK).transpose(1, 0, 2))
    return speeds, drift, stress


def iota(shape, dim):
    return lax.broadcasted_iota(jnp.int32, shape, dim)


def dot(a, b, dims=((1,), (0,)), precision=None):
    return lax.dot_general(
        a, b, (dims, ((), ())), precision=precision, preferred_element_type=F32
    )


def ones_where(cond, dtype=F32):
    return jnp.where(cond, 1.0, 0.0).astype(dtype)


def kernel(
    n,
    east_ref,
    north_ref,
    land_ref,
    energy_ref,
    win_ref,
    wout_ref,
    conv1_ref,
    conv2_ref,
    conv3_ref,
    speeds_ref,
    drift_ref,
    stress_ref,
    east_out,
    north_out,
    final_ref,
    first_ref,
    left_ref,
    right_ref,
    source_ref,
    hidden_ref,
    acc_ref,
    cur_ref,
    send_cur,
    recv_cur,
    send_for,
    recv_for,
    own_ref,
    up_ref,
    down_ref,
    taps1,
    taps2,
    drift_acc,
    drift_in,
    halo_send,
    halo_recv,
    cur_send_sem,
    cur_recv_sem,
    for_send_sem,
    for_recv_sem,
    ocean_send_sem,
    ocean_recv_sem,
):
    me = lax.axis_index("gx")
    has_left = me > 0
    has_right = me < n - 1
    rows, width = east_ref.shape
    wide = own_ref.shape[2]
    cells = cur_ref.shape[1]
    per_tile = LANES // rows
    tiles = cells // LANES

    barrier = pltpu.get_barrier_semaphore()

    @pl.loop(1, n)
    def _(d):
        peer = lax.rem(me + d, n)
        pl.semaphore_signal(barrier, inc=1, device_id={"gx": peer}, device_id_type=MESH)

    sea = land_ref[...].astype(F32)
    mu = east_ref[...] * sea
    mv = north_ref[...] * sea
    col = iota((width, 8 * n), 0)
    slot = iota((width, 8 * n), 1)
    peer_of = slot >> 3
    item = slot & 7
    pick_u = ones_where((item < 4) & (col == 2 * peer_of - 1 + item), BF16)
    pick_v = ones_where((item >= 4) & (item < 6) & (col == 2 * peer_of + item - 4), BF16)
    pick_m = ones_where((item >= 6) & (col == 2 * peer_of + item - 6), BF16)
    picked = (
        dot(mu.astype(BF16), pick_u) + dot(mv.astype(BF16), pick_v) + dot(sea.astype(BF16), pick_m)
    ).astype(BF16)
    offset = lax.rem(me * rows, LANES)
    place = iota((rows, LANES), 1) == iota((rows, LANES), 0) + offset
    blocks = dot(picked, ones_where(place, BF16), ((0,), (0,)))
    send_cur[...] = blocks.reshape(n, 8, LANES)
    recv_cur[pl.ds(me, 1)] = send_cur[pl.ds(me, 1)]
    own_ref[...] = jnp.zeros_like(own_ref)
    own_ref[0, :, :width] = mu
    own_ref[1, :, :width] = mv

    @pl.when(jnp.logical_not(has_left))
    def _():
        left_ref[...] = jnp.zeros_like(left_ref)
        up_ref[...] = jnp.zeros_like(up_ref)

    @pl.when(jnp.logical_not(has_right))
    def _():
        right_ref[...] = jnp.zeros_like(right_ref)
        down_ref[...] = jnp.zeros_like(down_ref)

    pl.semaphore_wait(barrier, n - 1)

    def current_copy(peer, d, sender):
        return pltpu.make_async_remote_copy(
            src_ref=send_cur.at[peer],
            dst_ref=recv_cur.at[sender],
            send_sem=cur_send_sem.at[d],
            recv_sem=cur_recv_sem.at[sender],
            device_id={"gx": peer},
            device_id_type=MESH,
        )

    def halo_copy(step, source, k, rightward):
        span = pl.ds(pl.multiple_of(k * CHUNK, CHUNK), CHUNK)
        side = 0 if rightward else 1
        target = left_ref if rightward else right_ref
        peer = lax.rem(me + 1, n) if rightward else lax.rem(me + n - 1, n)
        return pltpu.make_async_remote_copy(
            src_ref=source.at[1 if rightward else 0, span],
            dst_ref=target.at[step, span],
            send_sem=halo_send.at[step, side, k],
            recv_sem=halo_recv.at[step, side, k],
            device_id={"gx": peer},
            device_id_type=MESH,
        )

    def ocean_copy(downward):
        peer = lax.rem(me + 1, n) if downward else lax.rem(me + n - 1, n)
        side = 0 if downward else 1
        return pltpu.make_async_remote_copy(
            src_ref=own_ref.at[:, pl.ds(rows - 8 if downward else 0, 8)],
            dst_ref=up_ref if downward else down_ref,
            send_sem=ocean_send_sem.at[side],
            recv_sem=ocean_recv_sem.at[side],
            device_id={"gx": peer},
            device_id_type=MESH,
        )

    def forcing_copy(peer, d, sender):
        return pltpu.make_async_remote_copy(
            src_ref=send_for.at[lax.div(peer * rows, LANES)],
            dst_ref=recv_for.at[sender],
            send_sem=for_send_sem.at[d],
            recv_sem=for_recv_sem.at[sender],
            device_id={"gx": peer},
            device_id_type=MESH,
        )

    def send_halo(step, source, k):
        @pl.when(has_right)
        def _():
            halo_copy(step, source, k, True).start()

        @pl.when(has_left)
        def _():
            halo_copy(step, source, k, False).start()

    send_halo(0, energy_ref, 0)

    @pl.loop(1, n)
    def _(d):
        current_copy(lax.rem(me + d, n), d, me).start()

    @pl.when(has_right)
    def _():
        ocean_copy(True).start()

    @pl.when(has_left)
    def _():
        ocean_copy(False).start()

    @pl.loop(1, CHUNKS)
    def _(k):
        send_halo(0, energy_ref, k)

    for c in range(2):
        z = dot(win_ref[...], energy_ref[c], ((0,), (0,)))
        hidden_ref[0, c] = jax.nn.gelu(z).astype(BF16)
    acc_ref[...] = jnp.zeros_like(acc_ref)

    @pl.when(has_left)
    def _():
        ocean_copy(True).wait_recv()

    @pl.when(has_right)
    def _():
        ocean_copy(False).wait_recv()

    strip = rows + 8
    flat = strip * width
    lane = iota((wide, flat), 1)
    spread = ones_where((lane & (width - 1)) == iota((wide, flat), 0), BF16)
    ext_rows = rows + 16
    start = (iota((ext_rows, flat), 0) - 4) * width
    ahead = iota((ext_rows, flat), 1) - start
    chosen = (ahead >= 0) & (ahead < width)
    bends = []
    lines = []
    ext_r = iota((rows, ext_rows), 1)
    ext_c = iota((rows, ext_rows), 0)
    vertical = ones_where((ext_r == ext_c + 7) | (ext_r == ext_c + 9))
    side_r = iota((wide, wide), 0)
    side_c = iota((wide, wide), 1)
    horizontal = ones_where(
        ((side_r == side_c + 1) | (side_r == side_c - 1)) & (side_r < width) & (side_c < width)
    )
    for f in range(2):
        own = own_ref[f]
        ext = jnp.concatenate([up_ref[f], own, down_ref[f]], axis=0)
        line = dot((INPUT_SCALE * ext).astype(BF16), spread)
        lines.append(jnp.sum(jnp.where(chosen, line, 0.0), axis=0, keepdims=True))
        bends.append(
            dot(vertical, ext, precision=HIGHEST)
            + dot(own, horizontal, precision=HIGHEST)
            - 4.0 * own
        )
    sub = iota((8, flat), 0)
    line8 = jnp.where(sub == 0, lines[0], jnp.where(sub == 1, lines[1], 0.0))

    def shifted(x, dy, dx):
        shape = x.shape
        moved = dy * width + dx
        y = pltpu.roll(x, (-moved) % flat, 1) if moved else x
        if dx:
            at = (iota(shape, 1) & (width - 1)) + dx
            y = jnp.where((at >= 0) & (at < width), y, 0.0)
        return y

    taps = [(dy, dx) for dy in (-1, 0, 1) for dx in (-1, 0, 1)]
    for t, (dy, dx) in enumerate(taps):
        taps1[2 * t : 2 * t + 2] = shifted(line8, dy, dx)[0:2]
    h1 = dot(conv1_ref[...], taps1[0:18].astype(BF16), ((0,), (0,)))
    h1 = jnp.maximum(h1, 0.0).astype(BF16).astype(F32)
    at = iota(h1.shape, 1) + (me * rows - 4) * width
    h1 = jnp.where((at >= 0) & (at < n * rows * width), h1, 0.0)
    hc = h1.shape[0]
    for t, (dy, dx) in enumerate(taps):
        moved = shifted(h1, dy, dx)[:, 4 * width : (4 + rows) * width]
        taps2[hc * t : hc * t + hc] = moved.astype(BF16)
    h2 = jnp.maximum(dot(conv2_ref[...], taps2[...]), 0.0).astype(BF16)
    closure = dot(conv3_ref[...], h2)
    body = rows * width
    back = iota((body, wide), 0)
    gather = ones_where((back & (width - 1)) == iota((body, wide), 1))
    begun = iota((rows, body), 1) - iota((rows, body), 0) * width
    mine = (begun >= 0) & (begun < width)
    closures = [
        dot(jnp.where(mine, closure[f : f + 1], 0.0), gather, precision=HIGHEST) for f in range(2)
    ]
    mu_w, mv_w = own_ref[0], own_ref[1]
    east_part = mu_w + VISCOSITY * bends[0] + CORIOLIS * mv_w + closures[0]
    north_part = mv_w + VISCOSITY * bends[1] - CORIOLIS * mu_w + closures[1]
    east_out[...] = east_part[:, :width]
    north_out[...] = north_part[:, :width]

    @pl.loop(1, n)
    def _(d):
        sender = lax.rem(me + d, n)
        current_copy(me, d, sender).wait_recv()

    for t in range(tiles):
        cur_ref[:, t * LANES : (t + 1) * LANES] = jnp.sum(
            recv_cur[t * per_tile : (t + 1) * per_tile], axis=0
        )

    drift_acc[...] = jnp.zeros_like(drift_acc)

    def wave_chunk(step, source, target, k):
        base = pl.multiple_of(k * CHUNK, CHUNK)
        span = pl.ds(base, CHUNK)
        for c in range(2):
            source_ref[c] = dot(wout_ref[span], hidden_ref[step, c])

        @pl.when(has_left)
        def _():
            halo_copy(step, source, k, True).wait_recv()

        @pl.when(has_right)
        def _():
            halo_copy(step, source, k, False).wait_recv()

        first_lane = iota((BLOCK, cells), 1) == 0
        last_lane = iota((BLOCK, cells), 1) == cells - 1
        for i in range(CHUNK // BLOCK):
            part = pl.ds(pl.multiple_of(base + i * BLOCK, BLOCK), BLOCK)
            cx = speeds_ref[part, 0:1]
            cy = speeds_ref[part, 1:2]
            e = [
                left_ref[step, part].astype(F32),
                source[0, part].astype(F32),
                source[1, part].astype(F32),
                right_ref[step, part].astype(F32),
            ]
            s = [cx + cur_ref[q : q + 1] for q in range(4)]
            news = []
            for c in range(2):
                mid = e[c + 1]
                sy = cy + cur_ref[4 + c : 5 + c]
                ahead_flux = jnp.maximum(sy, 0.0) * mid
                back_flux = jnp.minimum(sy, 0.0) * mid
                from_before = jnp.where(first_lane, 0.0, pltpu.roll(ahead_flux, 1, 1))
                from_after = jnp.where(last_lane, 0.0, pltpu.roll(back_flux, cells - 1, 1))
                total = (
                    mid * (1.0 - jnp.abs(s[c + 1]) - jnp.abs(sy))
                    + jnp.maximum(s[c], 0.0) * e[c]
                    - jnp.minimum(s[c + 2], 0.0) * e[c + 2]
                    + from_before
                    - from_after
                    + SOURCE_STEP * source_ref[c, i * BLOCK : (i + 1) * BLOCK]
                )
                news.append(cur_ref[6 + c : 7 + c] * total)
            for c in range(2):
                if step == 0:
                    target[c, part] = news[c].astype(BF16)
                else:
                    drift_in[c, i * BLOCK : (i + 1) * BLOCK] = news[c].astype(BF16)
            if step == 1:
                target[part] = jnp.stack(news, axis=1).astype(BF16)

    @pl.loop(0, CHUNKS)
    def _(k):
        wave_chunk(0, energy_ref, first_ref, k)
        send_halo(1, first_ref, k)
        span = pl.ds(pl.multiple_of(k * CHUNK, CHUNK), CHUNK)
        for c in range(2):
            acc_ref[c] += dot(win_ref[span], first_ref[c, span], ((0,), (0,)))

    stress_rows = dot(stress_ref[...], wout_ref[...])
    stress_x = stress_rows[0:1] + stress_rows[1:2] + stress_rows[2:3]
    stress_y = stress_rows[3:4] + stress_rows[4:5] + stress_rows[5:6]
    sub8 = iota((8, stress_rows.shape[1]), 0)
    stress8 = jnp.where(sub8 == 0, stress_x, jnp.where(sub8 == 1, stress_y, 0.0))
    stresses = []
    for c in range(2):
        hidden = jax.nn.gelu(acc_ref[c]).astype(BF16)
        hidden_ref[1, c] = hidden
        stresses.append(dot(stress8, hidden.astype(F32), precision=HIGHEST))

    @pl.loop(0, CHUNKS)
    def _(k):
        wave_chunk(1, first_ref, final_ref, k)
        for c in range(2):
            drift_acc[c] += dot(drift_ref[k], drift_in[c])

    sub_f = iota((8, cells), 0)
    packed = jnp.zeros((8, cells), F32)
    for c in range(2):
        d = drift_acc[c]
        drift_x = d[0:1] + d[1:2] + d[2:3]
        drift_y = d[3:4] + d[4:5] + d[5:6]
        east_force = CORIOLIS * drift_y + stresses[c][0:1]
        north_force = stresses[c][1:2] - CORIOLIS * drift_x
        packed = jnp.where(sub_f == c, east_force, packed)
        packed = jnp.where(sub_f == 2 + c, north_force, packed)
    for t in range(tiles):
        send_for[t] = packed[:, t * LANES : (t + 1) * LANES]

    @pl.loop(1, n)
    def _(d):
        forcing_copy(lax.rem(me + d, n), d, me).start()

    recv_for[pl.ds(me, 1)] = send_for[pl.ds(lax.div(me * rows, LANES), 1)]

    @pl.loop(1, n)
    def _(d):
        current_copy(lax.rem(me + d, n), d, me).wait_send()

    @pl.when(has_right)
    def _():
        ocean_copy(True).wait_send()

    @pl.when(has_left)
    def _():
        ocean_copy(False).wait_send()

    @pl.loop(0, CHUNKS)
    def _(k):
        for step, source in ((0, energy_ref), (1, first_ref)):

            @pl.when(has_right)
            def _(step=step, source=source):
                halo_copy(step, source, k, True).wait_send()

            @pl.when(has_left)
            def _(step=step, source=source):
                halo_copy(step, source, k, False).wait_send()

    @pl.loop(1, n)
    def _(d):
        sender = lax.rem(me + d, n)
        forcing_copy(me, d, sender).wait_recv()

    arrived = recv_for[...].reshape(8 * n, LANES)
    lanes_to_rows = dot(ones_where(place), arrived, ((1,), (1,)), precision=HIGHEST)
    slot_r = iota((8 * n, width), 0)
    owner = slot_r >> 3
    which = slot_r & 7
    out_col = iota((8 * n, width), 1)
    east_pick = ones_where((which < 2) & (out_col == 2 * owner + which))
    north_pick = ones_where((which >= 2) & (which < 4) & (out_col == 2 * owner + which - 2))
    east_out[...] = sea * (east_out[...] + dot(lanes_to_rows, east_pick, precision=HIGHEST))
    north_out[...] = sea * (north_out[...] + dot(lanes_to_rows, north_pick, precision=HIGHEST))

    @pl.loop(1, n)
    def _(d):
        forcing_copy(lax.rem(me + d, n), d, me).wait_send()


def local(
    n,
    east_current,
    north_current,
    land_mask,
    spectrum,
    spectral_in,
    spectral_out,
    conv_first,
    conv_second,
    conv_last,
):
    rows, width = east_current.shape
    bins, columns, cells = spectrum.shape
    hid = spectral_in.shape[0]
    hc = conv_first.shape[0]
    assert columns == 2 and LANES % rows == 0 and rows >= 8
    assert width & (width - 1) == 0 and width % 32 == 0 and cells % LANES == 0
    wide = -(-width // LANES) * LANES
    speeds, drift, stress = bin_tables()
    vmem = pl.BlockSpec(memory_space=pltpu.VMEM)
    east, north, final = pl.pallas_call(
        functools.partial(kernel, n),
        out_shape=(
            jax.ShapeDtypeStruct((rows, width), F32),
            jax.ShapeDtypeStruct((rows, width), F32),
            jax.ShapeDtypeStruct((bins, columns, cells), BF16),
        ),
        in_specs=[vmem] * 12,
        out_specs=(vmem, vmem, vmem),
        scratch_shapes=[
            pltpu.VMEM((columns, bins, cells), BF16),
            pltpu.VMEM((2, bins, cells), BF16),
            pltpu.VMEM((2, bins, cells), BF16),
            pltpu.VMEM((columns, CHUNK, cells), F32),
            pltpu.VMEM((2, columns, hid, cells), BF16),
            pltpu.VMEM((columns, hid, cells), F32),
            pltpu.VMEM((8, cells), F32),
            pltpu.VMEM((n, 8, LANES), F32),
            pltpu.VMEM((n, 8, LANES), F32),
            pltpu.VMEM((cells // LANES, 8, LANES), F32),
            pltpu.VMEM((n, 8, LANES), F32),
            pltpu.VMEM((2, rows, wide), F32),
            pltpu.VMEM((2, 8, wide), F32),
            pltpu.VMEM((2, 8, wide), F32),
            pltpu.VMEM((24, (rows + 8) * width), F32),
            pltpu.VMEM((9 * hc, rows * width), BF16),
            pltpu.VMEM((columns, 16, cells), F32),
            pltpu.VMEM((columns, CHUNK, cells), BF16),
            pltpu.SemaphoreType.DMA((2, 2, CHUNKS)),
            pltpu.SemaphoreType.DMA((2, 2, CHUNKS)),
            pltpu.SemaphoreType.DMA((n,)),
            pltpu.SemaphoreType.DMA((n,)),
            pltpu.SemaphoreType.DMA((n,)),
            pltpu.SemaphoreType.DMA((n,)),
            pltpu.SemaphoreType.DMA((2,)),
            pltpu.SemaphoreType.DMA((2,)),
        ],
        compiler_params=pltpu.CompilerParams(
            collective_id=0, has_side_effects=True, vmem_limit_bytes=56 << 20
        ),
    )(
        east_current,
        north_current,
        land_mask,
        spectrum.transpose(1, 0, 2),
        spectral_in.T,
        spectral_out,
        conv_first.T,
        conv_second,
        conv_last,
        jnp.asarray(speeds),
        jnp.asarray(drift),
        jnp.asarray(stress),
    )
    return east, north, final


def solution(mesh):
    n = mesh.shape["gx"]
    in_specs = (
        P(("groups", "gx"), None),
        P(("groups", "gx"), None),
        P(("groups", "gx"), None),
        P(None, ("groups", "gx"), None),
        P(),
        P(),
        P(),
        P(),
        P(),
    )
    out_specs = (
        P(("groups", "gx"), None),
        P(("groups", "gx"), None),
        P(None, ("groups", "gx"), None),
    )
    return jax.shard_map(
        functools.partial(local, n), mesh=mesh, in_specs=in_specs, out_specs=out_specs, check_vma=False
    )
```

```python
import functools
import math

import jax
import jax.numpy as jnp
import ml_dtypes
import numpy as np
from jax import lax
from jax.experimental import pallas as pl
from jax.experimental.pallas import tpu as pltpu
from jax.sharding import PartitionSpec as P

DIRS = 36
FRQS = 36
BINS = DIRS * FRQS
VISCOSITY = 0.1
CORIOLIS = 0.3
INPUT_SCALE = 5.0
SOURCE_STEP = 1.0
SPEED_MAX = 0.25

CHUNKS = 9
CHUNK = BINS // CHUNKS
BLOCK = 16
LANES = 128
MESH = pl.DeviceIdType.MESH
F32 = jnp.float32
BF16 = jnp.bfloat16
HIGHEST = lax.Precision.HIGHEST


def split_rows(row):
    pieces = []
    rest = row.astype(np.float32)
    for _ in range(3):
        piece = rest.astype(ml_dtypes.bfloat16)
        pieces.append(piece)
        rest = rest - piece.astype(np.float32)
    return pieces


def bin_tables():
    index = np.arange(BINS)
    heading = (index // FRQS).astype(np.float64)
    level = (index % FRQS).astype(np.float64)
    theta = (heading + 0.5) * (2.0 * math.pi / DIRS)
    speed = SPEED_MAX * np.exp(-math.log(1.1) * level)
    factor = 2.0 / math.sqrt(BINS)
    cosine, sine = np.cos(theta), np.sin(theta)
    speeds = np.stack([speed * cosine, speed * sine], axis=1).astype(np.float32)
    weight = factor * (1.0 + level / FRQS)
    drift = np.zeros((16, BINS), ml_dtypes.bfloat16)
    drift[0:3] = split_rows(cosine * weight)
    drift[3:6] = split_rows(sine * weight)
    stress = np.zeros((16, BINS), ml_dtypes.bfloat16)
    stress[0:3] = split_rows(cosine * factor)
    stress[3:6] = split_rows(sine * factor)
    drift = np.ascontiguousarray(drift.reshape(16, CHUNKS, CHUNK).transpose(1, 0, 2))
    return speeds, drift, stress


def iota(shape, dim):
    return lax.broadcasted_iota(jnp.int32, shape, dim)


def dot(a, b, dims=((1,), (0,)), precision=None):
    return lax.dot_general(
        a, b, (dims, ((), ())), precision=precision, preferred_element_type=F32
    )


def ones_where(cond, dtype=F32):
    return jnp.where(cond, 1.0, 0.0).astype(dtype)


def kernel(
    n,
    east_ref,
    north_ref,
    land_ref,
    energy_ref,
    win_ref,
    wout_ref,
    conv1_ref,
    conv2_ref,
    conv3_ref,
    speeds_ref,
    drift_ref,
    stress_ref,
    both_out,
    final_ref,
    first_ref,
    left_ref,
    right_ref,
    source_ref,
    hidden_ref,
    acc_ref,
    cur_ref,
    send_cur,
    recv_cur,
    send_for,
    recv_for,
    own_ref,
    up_ref,
    down_ref,
    taps1,
    taps2,
    drift_acc,
    drift_in,
    halo_send,
    halo_recv,
    cur_send_sem,
    cur_recv_sem,
    for_send_sem,
    for_recv_sem,
    ocean_send_sem,
    ocean_recv_sem,
):
    me = lax.axis_index("gx")
    east_out, north_out = both_out.at[0], both_out.at[1]
    has_left = me > 0
    has_right = me < n - 1
    rows, width = east_ref.shape
    wide = own_ref.shape[2]
    cells = cur_ref.shape[1]
    per_tile = LANES // rows
    tiles = cells // LANES

    barrier = pltpu.get_barrier_semaphore()

    @pl.loop(1, n, unroll=True)
    def _(d):
        peer = lax.rem(me + d, n)
        pl.semaphore_signal(barrier, inc=1, device_id={"gx": peer}, device_id_type=MESH)

    sea = land_ref[...].astype(F32)
    mu = east_ref[...] * sea
    mv = north_ref[...] * sea
    col = iota((width, 8 * n), 0)
    slot = iota((width, 8 * n), 1)
    peer_of = slot >> 3
    item = slot & 7
    pick_u = ones_where((item < 4) & (col == 2 * peer_of - 1 + item), BF16)
    pick_v = ones_where((item >= 4) & (item < 6) & (col == 2 * peer_of + item - 4), BF16)
    pick_m = ones_where((item >= 6) & (col == 2 * peer_of + item - 6), BF16)
    picked = (
        dot(mu.astype(BF16), pick_u) + dot(mv.astype(BF16), pick_v) + dot(sea.astype(BF16), pick_m)
    ).astype(BF16)
    offset = lax.rem(me * rows, LANES)
    place = iota((rows, LANES), 1) == iota((rows, LANES), 0) + offset
    blocks = dot(picked, ones_where(place, BF16), ((0,), (0,)))
    send_cur[...] = blocks.reshape(n, 8, LANES)
    recv_cur[pl.ds(me, 1)] = send_cur[pl.ds(me, 1)]
    own_ref[...] = jnp.zeros_like(own_ref)
    own_ref[0, :, :width] = mu
    own_ref[1, :, :width] = mv

    @pl.when(jnp.logical_not(has_left))
    def _():
        left_ref[...] = jnp.zeros_like(left_ref)
        up_ref[...] = jnp.zeros_like(up_ref)

    @pl.when(jnp.logical_not(has_right))
    def _():
        right_ref[...] = jnp.zeros_like(right_ref)
        down_ref[...] = jnp.zeros_like(down_ref)

    pl.semaphore_wait(barrier, n - 1)

    def current_copy(peer, d, sender):
        return pltpu.make_async_remote_copy(
            src_ref=send_cur.at[peer],
            dst_ref=recv_cur.at[sender],
            send_sem=cur_send_sem.at[d],
            recv_sem=cur_recv_sem.at[sender],
            device_id={"gx": peer},
            device_id_type=MESH,
        )

    def halo_copy(step, source, k, rightward):
        span = pl.ds(pl.multiple_of(k * CHUNK, CHUNK), CHUNK)
        side = 0 if rightward else 1
        target = left_ref if rightward else right_ref
        peer = lax.rem(me + 1, n) if rightward else lax.rem(me + n - 1, n)
        return pltpu.make_async_remote_copy(
            src_ref=source.at[1 if rightward else 0, span],
            dst_ref=target.at[step, span],
            send_sem=halo_send.at[step, side, k],
            recv_sem=halo_recv.at[step, side, k],
            device_id={"gx": peer},
            device_id_type=MESH,
        )

    def ocean_copy(downward):
        peer = lax.rem(me + 1, n) if downward else lax.rem(me + n - 1, n)
        side = 0 if downward else 1
        return pltpu.make_async_remote_copy(
            src_ref=own_ref.at[:, pl.ds(rows - 8 if downward else 0, 8)],
            dst_ref=up_ref if downward else down_ref,
            send_sem=ocean_send_sem.at[side],
            recv_sem=ocean_recv_sem.at[side],
            device_id={"gx": peer},
            device_id_type=MESH,
        )

    def forcing_copy(peer, d, sender):
        return pltpu.make_async_remote_copy(
            src_ref=send_for.at[lax.div(peer * rows, LANES)],
            dst_ref=recv_for.at[sender],
            send_sem=for_send_sem.at[d],
            recv_sem=for_recv_sem.at[sender],
            device_id={"gx": peer},
            device_id_type=MESH,
        )

    def send_halo(step, source, k):
        @pl.when(has_right)
        def _():
            halo_copy(step, source, k, True).start()

        @pl.when(has_left)
        def _():
            halo_copy(step, source, k, False).start()

    @pl.loop(1, n, unroll=True)
    def _(d):
        current_copy(lax.rem(me + d, n), d, me).start()

    send_halo(0, energy_ref, 0)

    @pl.when(has_right)
    def _():
        ocean_copy(True).start()

    @pl.when(has_left)
    def _():
        ocean_copy(False).start()

    @pl.loop(1, CHUNKS)
    def _(k):
        send_halo(0, energy_ref, k)

    for c in range(2):
        z = dot(win_ref[...], energy_ref[c], ((0,), (0,)))
        hidden_ref[0, c] = jax.nn.gelu(z).astype(BF16)
    acc_ref[...] = jnp.zeros_like(acc_ref)

    @pl.loop(1, n, unroll=True)
    def _(d):
        sender = lax.rem(me + d, n)
        current_copy(me, d, sender).wait_recv()

    for t in range(tiles):
        cur_ref[:, t * LANES : (t + 1) * LANES] = jnp.sum(
            recv_cur[t * per_tile : (t + 1) * per_tile], axis=0
        )

    drift_acc[...] = jnp.zeros_like(drift_acc)

    def wave_chunk(step, source, target, k):
        base = pl.multiple_of(k * CHUNK, CHUNK)
        span = pl.ds(base, CHUNK)
        for c in range(2):
            source_ref[c] = dot(wout_ref[span], hidden_ref[step, c])

        @pl.when(has_left)
        def _():
            halo_copy(step, source, k, True).wait_recv()

        @pl.when(has_right)
        def _():
            halo_copy(step, source, k, False).wait_recv()

        first_lane = iota((BLOCK, cells), 1) == 0
        last_lane = iota((BLOCK, cells), 1) == cells - 1
        for i in range(CHUNK // BLOCK):
            part = pl.ds(pl.multiple_of(base + i * BLOCK, BLOCK), BLOCK)
            cx = speeds_ref[part, 0:1]
            cy = speeds_ref[part, 1:2]
            e = [
                left_ref[step, part].astype(F32),
                source[0, part].astype(F32),
                source[1, part].astype(F32),
                right_ref[step, part].astype(F32),
            ]
            s = [cx + cur_ref[q : q + 1] for q in range(4)]
            news = []
            for c in range(2):
                mid = e[c + 1]
                sy = cy + cur_ref[4 + c : 5 + c]
                ahead_flux = jnp.maximum(sy, 0.0) * mid
                back_flux = jnp.minimum(sy, 0.0) * mid
                from_before = jnp.where(first_lane, 0.0, pltpu.roll(ahead_flux, 1, 1))
                from_after = jnp.where(last_lane, 0.0, pltpu.roll(back_flux, cells - 1, 1))
                total = (
                    mid * (1.0 - jnp.abs(s[c + 1]) - jnp.abs(sy))
                    + jnp.maximum(s[c], 0.0) * e[c]
                    - jnp.minimum(s[c + 2], 0.0) * e[c + 2]
                    + from_before
                    - from_after
                    + SOURCE_STEP * source_ref[c, i * BLOCK : (i + 1) * BLOCK]
                )
                news.append(cur_ref[6 + c : 7 + c] * total)
            for c in range(2):
                if step == 0:
                    target[c, part] = news[c].astype(BF16)
                else:
                    drift_in[c, i * BLOCK : (i + 1) * BLOCK] = news[c].astype(BF16)
            if step == 1:
                target[part] = jnp.stack(news, axis=1).astype(BF16)

    @pl.loop(0, CHUNKS)
    def _(k):
        wave_chunk(0, energy_ref, first_ref, k)
        send_halo(1, first_ref, k)
        span = pl.ds(pl.multiple_of(k * CHUNK, CHUNK), CHUNK)
        for c in range(2):
            acc_ref[c] += dot(win_ref[span], first_ref[c, span], ((0,), (0,)))

    stress_rows = dot(stress_ref[...], wout_ref[...])
    stress_x = stress_rows[0:1] + stress_rows[1:2] + stress_rows[2:3]
    stress_y = stress_rows[3:4] + stress_rows[4:5] + stress_rows[5:6]
    sub8 = iota((8, stress_rows.shape[1]), 0)
    stress8 = jnp.where(sub8 == 0, stress_x, jnp.where(sub8 == 1, stress_y, 0.0))
    stresses = []
    for c in range(2):
        hidden = jax.nn.gelu(acc_ref[c]).astype(BF16)
        hidden_ref[1, c] = hidden
        stresses.append(dot(stress8, hidden.astype(F32), precision=HIGHEST))

    @pl.when(has_left)
    def _():
        ocean_copy(True).wait_recv()

    @pl.when(has_right)
    def _():
        ocean_copy(False).wait_recv()

    strip = rows + 8
    flat = strip * width
    lane = iota((wide, flat), 1)
    spread = ones_where((lane & (width - 1)) == iota((wide, flat), 0), BF16)
    ext_rows = rows + 16
    start = (iota((ext_rows, flat), 0) - 4) * width
    ahead = iota((ext_rows, flat), 1) - start
    chosen = (ahead >= 0) & (ahead < width)
    bends = []
    lines = []
    ext_r = iota((rows, ext_rows), 1)
    ext_c = iota((rows, ext_rows), 0)
    vertical = ones_where((ext_r == ext_c + 7) | (ext_r == ext_c + 9))
    side_r = iota((wide, wide), 0)
    side_c = iota((wide, wide), 1)
    horizontal = ones_where(
        ((side_r == side_c + 1) | (side_r == side_c - 1)) & (side_r < width) & (side_c < width)
    )
    for f in range(2):
        own = own_ref[f]
        ext = jnp.concatenate([up_ref[f], own, down_ref[f]], axis=0)
        line = dot((INPUT_SCALE * ext).astype(BF16), spread)
        lines.append(jnp.sum(jnp.where(chosen, line, 0.0), axis=0, keepdims=True))
        bends.append(
            dot(vertical, ext, precision=HIGHEST)
            + dot(own, horizontal, precision=HIGHEST)
            - 4.0 * own
        )
    sub = iota((8, flat), 0)
    line8 = jnp.where(sub == 0, lines[0], jnp.where(sub == 1, lines[1], 0.0))

    def shifted(x, dy, dx):
        shape = x.shape
        moved = dy * width + dx
        y = pltpu.roll(x, (-moved) % flat, 1) if moved else x
        if dx:
            at = (iota(shape, 1) & (width - 1)) + dx
            y = jnp.where((at >= 0) & (at < width), y, 0.0)
        return y

    taps = [(dy, dx) for dy in (-1, 0, 1) for dx in (-1, 0, 1)]
    for t, (dy, dx) in enumerate(taps):
        taps1[2 * t : 2 * t + 2] = shifted(line8, dy, dx)[0:2]
    h1 = dot(conv1_ref[...], taps1[0:18].astype(BF16), ((0,), (0,)))
    h1 = jnp.maximum(h1, 0.0).astype(BF16).astype(F32)
    at = iota(h1.shape, 1) + (me * rows - 4) * width
    h1 = jnp.where((at >= 0) & (at < n * rows * width), h1, 0.0)
    hc = h1.shape[0]
    for t, (dy, dx) in enumerate(taps):
        moved = shifted(h1, dy, dx)[:, 4 * width : (4 + rows) * width]
        taps2[hc * t : hc * t + hc] = moved.astype(BF16)
    h2 = jnp.maximum(dot(conv2_ref[...], taps2[...]), 0.0).astype(BF16)
    closure = dot(conv3_ref[...], h2)
    body = rows * width
    back = iota((body, wide), 0)
    gather = ones_where((back & (width - 1)) == iota((body, wide), 1))
    begun = iota((rows, body), 1) - iota((rows, body), 0) * width
    mine = (begun >= 0) & (begun < width)
    closures = [
        dot(jnp.where(mine, closure[f : f + 1], 0.0), gather, precision=HIGHEST) for f in range(2)
    ]
    mu_w, mv_w = own_ref[0], own_ref[1]
    east_part = mu_w + VISCOSITY * bends[0] + CORIOLIS * mv_w + closures[0]
    north_part = mv_w + VISCOSITY * bends[1] - CORIOLIS * mu_w + closures[1]
    east_out[...] = east_part[:, :width]
    north_out[...] = north_part[:, :width]

    @pl.loop(0, CHUNKS)
    def _(k):
        wave_chunk(1, first_ref, final_ref, k)
        for c in range(2):
            drift_acc[c] += dot(drift_ref[k], drift_in[c])

    sub_f = iota((8, cells), 0)
    packed = jnp.zeros((8, cells), F32)
    for c in range(2):
        d = drift_acc[c]
        drift_x = d[0:1] + d[1:2] + d[2:3]
        drift_y = d[3:4] + d[4:5] + d[5:6]
        east_force = CORIOLIS * drift_y + stresses[c][0:1]
        north_force = stresses[c][1:2] - CORIOLIS * drift_x
        packed = jnp.where(sub_f == c, east_force, packed)
        packed = jnp.where(sub_f == 2 + c, north_force, packed)
    for t in range(tiles):
        send_for[t] = packed[:, t * LANES : (t + 1) * LANES]

    @pl.loop(1, n, unroll=True)
    def _(d):
        forcing_copy(lax.rem(me + d, n), d, me).start()

    recv_for[pl.ds(me, 1)] = send_for[pl.ds(lax.div(me * rows, LANES), 1)]

    @pl.loop(1, n, unroll=True)
    def _(d):
        current_copy(lax.rem(me + d, n), d, me).wait_send()

    @pl.when(has_right)
    def _():
        ocean_copy(True).wait_send()

    @pl.when(has_left)
    def _():
        ocean_copy(False).wait_send()

    @pl.loop(0, CHUNKS)
    def _(k):
        for step, source in ((0, energy_ref), (1, first_ref)):

            @pl.when(has_right)
            def _(step=step, source=source):
                halo_copy(step, source, k, True).wait_send()

            @pl.when(has_left)
            def _(step=step, source=source):
                halo_copy(step, source, k, False).wait_send()

    @pl.loop(1, n, unroll=True)
    def _(d):
        sender = lax.rem(me + d, n)
        forcing_copy(me, d, sender).wait_recv()

    arrived = recv_for[...].reshape(8 * n, LANES)
    lanes_to_rows = dot(ones_where(place), arrived, ((1,), (1,)), precision=HIGHEST)
    slot_r = iota((8 * n, width), 0)
    owner = slot_r >> 3
    which = slot_r & 7
    out_col = iota((8 * n, width), 1)
    east_pick = ones_where((which < 2) & (out_col == 2 * owner + which))
    north_pick = ones_where((which >= 2) & (which < 4) & (out_col == 2 * owner + which - 2))
    east_out[...] = sea * (east_out[...] + dot(lanes_to_rows, east_pick, precision=HIGHEST))
    north_out[...] = sea * (north_out[...] + dot(lanes_to_rows, north_pick, precision=HIGHEST))

    @pl.loop(1, n, unroll=True)
    def _(d):
        forcing_copy(lax.rem(me + d, n), d, me).wait_send()


def local(
    n,
    east_current,
    north_current,
    land_mask,
    spectrum,
    spectral_in,
    spectral_out,
    conv_first,
    conv_second,
    conv_last,
):
    rows, width = east_current.shape
    bins, columns, cells = spectrum.shape
    hid = spectral_in.shape[0]
    hc = conv_first.shape[0]
    assert columns == 2 and LANES % rows == 0 and rows >= 8
    assert width & (width - 1) == 0 and width % 32 == 0 and cells % LANES == 0
    wide = -(-width // LANES) * LANES
    speeds, drift, stress = bin_tables()
    vmem = pl.BlockSpec(memory_space=pltpu.VMEM)
    both, final = pl.pallas_call(
        functools.partial(kernel, n),
        out_shape=(
            jax.ShapeDtypeStruct((2, rows, width), F32),
            jax.ShapeDtypeStruct((bins, columns, cells), BF16),
        ),
        in_specs=[vmem] * 12,
        out_specs=(vmem, vmem),
        scratch_shapes=[
            pltpu.VMEM((columns, bins, cells), BF16),
            pltpu.VMEM((2, bins, cells), BF16),
            pltpu.VMEM((2, bins, cells), BF16),
            pltpu.VMEM((columns, CHUNK, cells), F32),
            pltpu.VMEM((2, columns, hid, cells), BF16),
            pltpu.VMEM((columns, hid, cells), F32),
            pltpu.VMEM((8, cells), F32),
            pltpu.VMEM((n, 8, LANES), F32),
            pltpu.VMEM((n, 8, LANES), F32),
            pltpu.VMEM((cells // LANES, 8, LANES), F32),
            pltpu.VMEM((n, 8, LANES), F32),
            pltpu.VMEM((2, rows, wide), F32),
            pltpu.VMEM((2, 8, wide), F32),
            pltpu.VMEM((2, 8, wide), F32),
            pltpu.VMEM((24, (rows + 8) * width), F32),
            pltpu.VMEM((9 * hc, rows * width), BF16),
            pltpu.VMEM((columns, 16, cells), F32),
            pltpu.VMEM((columns, CHUNK, cells), BF16),
            pltpu.SemaphoreType.DMA((2, 2, CHUNKS)),
            pltpu.SemaphoreType.DMA((2, 2, CHUNKS)),
            pltpu.SemaphoreType.DMA((n,)),
            pltpu.SemaphoreType.DMA((n,)),
            pltpu.SemaphoreType.DMA((n,)),
            pltpu.SemaphoreType.DMA((n,)),
            pltpu.SemaphoreType.DMA((2,)),
            pltpu.SemaphoreType.DMA((2,)),
        ],
        compiler_params=pltpu.CompilerParams(
            collective_id=0, has_side_effects=True, vmem_limit_bytes=20 * bins * cells + (16 << 20)
        ),
    )(
        east_current,
        north_current,
        land_mask,
        spectrum.transpose(1, 0, 2),
        spectral_in.T,
        spectral_out,
        conv_first.T,
        conv_second,
        conv_last,
        jnp.asarray(speeds),
        jnp.asarray(drift),
        jnp.asarray(stress),
    )
    return both[0], both[1], final


def solution(mesh):
    n = mesh.shape["gx"]
    in_specs = (
        P(("groups", "gx"), None),
        P(("groups", "gx"), None),
        P(("groups", "gx"), None),
        P(None, ("groups", "gx"), None),
        P(),
        P(),
        P(),
        P(),
        P(),
    )
    out_specs = (
        P(("groups", "gx"), None),
        P(("groups", "gx"), None),
        P(None, ("groups", "gx"), None),
    )
    return jax.shard_map(
        functools.partial(local, n), mesh=mesh, in_specs=in_specs, out_specs=out_specs, check_vma=False
    )
```
